512 devices in a mesh: kcol: 128 (over y, z, core), band: 4 (over x).
Axes of the slice: x: 4, y: 4, z: 16, core: 2. Of those that a mesh axis runs over, the one named last changes fastest.
Arguments:
- coarse_kernel: bfloat16 [576, 73728], P('band', 'kcol'), may hold values from -6 to 6
- row_intersection: float32 [2, 4, 8, 12], P(None, 'band'), may hold values from -1.75 to 1.75
- col_intersection: float32 [2, 18432, 8, 12], P(None, 'kcol'), may hold values from -1.75 to 1.75
- row_nearest: int32 [4], P('band'), may hold values from 0 to 3
- col_nearest: int32 [18432], P('kcol'), may hold values from 0 to 511, as said below
- qp_energy: float32 [256], P('band'), may hold values from 1 to 4
Outputs:
- fine_kernel: bfloat16 [256, 1179648], P('band', 'kcol')
The draws below stay inside these ranges and needn't reach their ends.
Inputs may be any that keep to these rules, and one draw needn't show every extreme that they name: `col_nearest`: coarse point c is held by index c // 4 of kcol. Among the 144 fine points held by one index of kcol, at most 2 have nearest coarse points held by any one index of kcol; in every draw one index of kcol is the holder for exactly 2 fine points of every index.
All inputs are finite; a program needn't handle non-finite values.
Results may differ from the reference program's by a relative error of at most 0.0012.
The reference program's roundings to bfloat16 on the way count: a program that leaves them out, or rounds other values in their place, can miss the bound.
Values may be sent and summed in bfloat16 or wider, within the bound.
No kernel may reach another device: no remote copies, remote signals or barrier semaphores. Data moves between devices by JAX's collectives and lax.ppermute only.
A program may use at most 192 MiB of HBM per device.

```python
import jax
import jax.numpy as jnp
from jax import lax

NBF = 8
NBC = 12
RC = 4
ROWS = 4
FC_DEV = 144
CC_DEV = 4
FINE = 18432
COARSE = 512
CAP = 2
N_KCOL = 128


def draw_col_nearest(key, part):
    key = jax.random.fold_in(key, 11)
    first_key, second_key = jax.random.split(key, 2)
    busiest = jax.random.randint(first_key, (), 0, N_KCOL)
    slots = CAP * N_KCOL

    def one_device(device_key):
        order_key, shuffle_key, local_key = jax.random.split(device_key, 3)
        order = jax.random.permutation(order_key, slots)
        holder = jnp.arange(slots, dtype=jnp.int32) % N_KCOL
        score = order + jnp.where(holder == busiest, -slots, 0)
        picked = jnp.argsort(score)[:FC_DEV]
        holders = (picked % N_KCOL).astype(jnp.int32)
        holders = holders[jax.random.permutation(shuffle_key, FC_DEV)]
        local = jax.random.randint(local_key, (FC_DEV,), 0, CC_DEV)
        return (holders * CC_DEV + local).astype(jnp.int32)
    device_keys = jax.random.split(second_key, N_KCOL)
    return jax.vmap(one_device)(device_keys).reshape(FC_DEV * N_KCOL)


def plant(entries, stream_key, low, high):
    extent = entries.shape
    index_at = [jax.random.randint(jax.random.fold_in(stream_key, axis), (), 0, extent[axis]) for axis in range(len(extent))]
    entries = entries.at[tuple(index_at)].set(low)
    longest = extent.index(max(extent))
    index_at[longest] = (index_at[longest] + 1) % extent[longest]
    return entries.at[tuple(index_at)].set(high)


def levels(own_key, dims, shards, low, largest):
    def one(dim, parts):
        draws = jax.random.uniform(jax.random.fold_in(jax.random.fold_in(own_key, 6), dim), (parts,), jnp.float32, low / len(shards), largest / len(shards))
        return jnp.repeat(jnp.exp(draws), dims[dim] // parts).reshape((-1,) + (1,) * (len(dims) - dim - 1))

    factor_of = one(*shards[0])
    for cut in shards[1:]:
        factor_of = factor_of * one(*cut)
    return factor_of


def gaussian(stream_key, dims, spread, bound, shards=(), kind=jnp.bfloat16):
    drawn = spread * jax.random.normal(stream_key, dims, jnp.float32)
    if shards:
        drawn = drawn * levels(stream_key, dims, shards, -0.22, 0.18)
    return jnp.clip(drawn, -bound, bound).astype(kind)


def setup_inputs(seed: int = 0) -> dict:
    key_of = jax.random.split(jax.random.key(seed), 7)
    return {
        "coarse_kernel": gaussian(key_of[0], (RC * NBC * NBC, COARSE * NBC * NBC), 1.0, 6.0, ((0, 4), (1, 128))),
        "row_intersection": gaussian(key_of[1], (2, ROWS, NBF, NBC), NBC ** -0.5, 1.75, ((1, 4),), jnp.float32),
        "col_intersection": gaussian(key_of[2], (2, FINE, NBF, NBC), NBC ** -0.5, 1.75, ((1, 128),), jnp.float32),
        "row_nearest": plant(jax.random.randint(key_of[3], (ROWS,), 0, RC), jax.random.fold_in(key_of[3], 1), 0, RC - 1).astype(jnp.int32),
        "col_nearest": draw_col_nearest(jax.random.fold_in(key_of[6], 71), 0),
        "qp_energy": jnp.clip(1.0 + 3.0 * jax.random.uniform(key_of[5], (ROWS * NBF * NBF,), jnp.float32) ** levels(key_of[5], (ROWS * NBF * NBF,), ((0, 4),), -0.2, 0.2), 1.0, 4.0),
    }


def pair_coefficient(intersection):
    conduction = intersection[0]
    valence = intersection[1]
    points = conduction.shape[0]
    fine_bands = conduction.shape[1]
    coarse_bands = conduction.shape[2]
    product = conduction[:, :, None, :, None] * valence[:, None, :, None, :]
    return product.reshape(points, fine_bands * fine_bands, coarse_bands * coarse_bands)


def reference(coarse_kernel, row_intersection, col_intersection, row_nearest, col_nearest, qp_energy):
    fine_pairs = NBF * NBF
    coarse_pairs = NBC * NBC
    row_coef = pair_coefficient(row_intersection).astype(jnp.bfloat16)
    col_coef = pair_coefficient(col_intersection).astype(jnp.bfloat16)
    blocks = coarse_kernel.reshape(RC, coarse_pairs, COARSE * coarse_pairs)

    def one_row(inputs):
        coefficient, nearest = inputs
        rows = lax.dynamic_index_in_dim(blocks, nearest, 0, keepdims=False)
        return jnp.dot(coefficient, rows, preferred_element_type=jnp.float32).astype(jnp.bfloat16)

    strip = lax.map(one_row, (row_coef, row_nearest))
    all_rows = ROWS * fine_pairs
    strip = strip.reshape(all_rows, COARSE, coarse_pairs)
    block_coef = col_coef.reshape(N_KCOL, FC_DEV, fine_pairs, coarse_pairs)
    block_near = col_nearest.reshape(N_KCOL, FC_DEV)
    width = FC_DEV * fine_pairs

    def one_block(index, output):
        coefficient = lax.dynamic_index_in_dim(block_coef, index, 0, keepdims=False)
        nearest = lax.dynamic_index_in_dim(block_near, index, 0, keepdims=False)
        picked = jnp.take(strip, nearest, axis=1)
        result = jnp.einsum("rjq,jpq->rjp", picked.astype(jnp.float32), coefficient.astype(jnp.float32))
        result = result.reshape(all_rows, width).astype(jnp.bfloat16)
        start = (index * width).astype(jnp.int32)
        return lax.dynamic_update_slice(output, result, (jnp.zeros((), jnp.int32), start))

    output = jnp.zeros((all_rows, FINE * fine_pairs), jnp.bfloat16)
    output = lax.fori_loop(0, N_KCOL, one_block, output)
    head = output[:, :all_rows].astype(jnp.float32) + jnp.diag(qp_energy)
    return output.at[:, :all_rows].set(head.astype(jnp.bfloat16))
```

```python
import jax
import jax.numpy as jnp
from jax import lax
from jax.experimental import pallas as pl
from jax.experimental.pallas import tpu as pltpu
from jax.sharding import Mesh
from jax.sharding import PartitionSpec as P

NBF = 8
NBC = 12
FP = NBF * NBF
CP = NBC * NBC
RC = 4
NY, NZ, NC, NB = 4, 16, 2, 4
GROUP = NY * NC
FC = 144
HELD = 4
CAP = 2
REL = (0, -1, 1, -2, -3, 2, 3, -4, -5, 4, 5, -6, -7, 6, 7, 8)
F32 = jnp.float32
BF16 = jnp.bfloat16


def iota(shape, dim):
    return lax.broadcasted_iota(jnp.int32, shape, dim)


def dot(a, b, dims=((1,), (0,))):
    return lax.dot_general(a, b, (dims, ((), ())), preferred_element_type=F32)


def whole(n):
    return [pl.BlockSpec(memory_space=pltpu.VMEM)] * n


def strip_kernel(pick_ref, k0, k1, k2, k3, coef_ref, out_ref):
    pick = pick_ref[0]
    rows = jnp.where(pick == 0, k0[...], k1[...])
    rows = jnp.where(pick == 2, k2[...], rows)
    rows = jnp.where(pick == 3, k3[...], rows)
    strip = dot(rows, coef_ref[...], ((0,), (1,))).astype(BF16)
    to = iota((CP, CP), 0)
    low = (to >> 3) * NBC + (to & 7)
    high = ((to - 96) >> 2) * NBC + 8 + (to & 3)
    order = (jnp.where(to < 96, low, high) == iota((CP, CP), 1)).astype(BF16)
    for pair in range(2):
        at = pair * 2 * CP
        both = jnp.concatenate([strip[at : at + CP], strip[at + CP : at + 2 * CP]], axis=1)
        out_ref[pair] = dot(order, both).astype(BF16)


def request_kernel(z_ref, row_ref, col_ref, conduction_ref, valence_ref, out_ref, slot_ref):
    z = z_ref[0]
    near = row_ref[...]
    holder = near >> 2
    earlier = ((col_ref[...] >> 2) == holder) & (iota((FC, FC), 0) < iota((FC, FC), 1))
    rank = jnp.sum(earlier.astype(jnp.int32), axis=0, keepdims=True)
    rel = ((holder >> 1) - z) & (NZ - 1)
    pos = jnp.zeros_like(rel)
    for k, offset in enumerate(REL):
        pos = jnp.where(rel == (offset % NZ), k, pos)
    group = (holder >> 5) * NC + (holder & 1)
    slot = (group * NZ + pos) * CAP + rank
    slot_ref[...] = slot
    lanes = 12 * 64
    source = iota((96, lanes), 0)
    lane = iota((96, lanes), 1)
    i, inner = lane >> 6, lane & 63
    spot = (inner & 7) * NBC + i
    table = jnp.zeros((FC, lanes), F32)
    for t, ref in enumerate((conduction_ref, valence_ref)):
        rest = ref[...]
        for s in range(3):
            term = rest.astype(BF16)
            rest = rest - term.astype(F32)
            place = ((source == spot) & ((inner >> 3) == s * 2 + t)).astype(BF16)
            table = table + dot(term, place)
    local = (col_ref[...] & 3).astype(F32)
    table = jnp.where((iota((FC, lanes), 1) & 63) == 48, local, table).astype(BF16)
    row = iota((GROUP * NZ, FC), 0) * CAP
    for r in range(CAP):
        one = (slot == row + r).astype(BF16)
        out_ref[:, r] = dot(one, table).astype(BF16).reshape(GROUP, NZ, lanes)


def expand_kernel(x_ref, u_ref, v_ref, local_ref):
    k = iota((256, 512), 0)
    n = iota((256, 512), 1)
    inner = k & 63
    want = jnp.where((n & 128) == 0, (n >> 3) & 7, n & 7)
    same = ((k >> 7) == ((n >> 6) & 1)) & (((k >> 6) & 1) == (n >> 8))
    same = same & (inner < 48) & (((inner >> 3) & 1) == ((n >> 7) & 1)) & ((inner & 7) == want)
    spread = same.astype(BF16)
    k = iota((256, 128), 0)
    n = iota((256, 128), 1)
    spread_local = (((k & 127) == 48) & ((k >> 7) == (n >> 6))).astype(BF16)
    for d in range(GROUP):
        lanes = pl.ds(d * 128, 128)
        for m in range(6):
            at = pl.ds(m * 128, 128)
            x = jnp.concatenate([x_ref[d, 0, :, at], x_ref[d, 1, :, at]], axis=1)
            y = dot(x, spread)
            for half in range(2):
                rows = pl.ds((m * 2 + half) * NZ, NZ)
                u_ref[d, rows] = y[:, half * 256 : half * 256 + 128]
                v_ref[d, rows] = y[:, half * 256 + 128 : half * 256 + 256]
            if m == 0:
                local_ref[:, lanes] = dot(x, spread_local)


def coefficients(u_ref, v_ref, d, pos):
    u = [jnp.broadcast_to(u_ref[d, pl.ds(i * NZ + pos, 1)], (8, 128)) for i in range(NBC)]
    v_low = v_ref[d, pl.ds(pos, 8, stride=NZ)]
    v_high = v_ref[d, pl.ds(8 * NZ + pos, 4, stride=NZ)]
    v_high = jnp.concatenate([v_high, v_high], axis=0)
    first = iota((8, 128), 0) < 4
    parts = [v_low * u[i] for i in range(NBC)]
    parts += [v_high * jnp.where(first, u[i], u[i + 1]) for i in range(0, NBC, 2)]
    return jnp.concatenate(parts, axis=0).astype(BF16)


def result_kernel(places, u_ref, v_ref, local_ref, *refs):
    strips, out_ref = refs[:-1], refs[-1]
    for at, (pos, pairs) in enumerate(places):
        blocks = [strips[a][b] for a, b in pairs]
        for chunk in range(4):
            lanes = pl.ds(chunk * 256, 256)
            coef = jnp.concatenate([coefficients(u_ref, v_ref, 2 * chunk + d, pos) for d in range(2)], axis=1)
            low = dot(blocks[0], coef, ((0,), (0,)))
            high = dot(blocks[1], coef, ((0,), (0,)))
            local = local_ref[pl.ds(pos, 1), lanes]
            res = jnp.where(local == 0, low[:FP], low[FP:])
            res = jnp.where(local == 2, high[:FP], res)
            res = jnp.where(local == 3, high[FP:], res).astype(BF16)
            for half in range(2):
                out_ref[chunk * 2 + half, at] = res[:, half * 128 : half * 128 + 128]


def assemble_kernel(slot_ref, where_ref, got_ref, qp_ref, out_ref):
    step = pl.program_id(0)
    tiles = out_ref.shape[1] // 128
    first = where_ref[0]
    lane = iota((FP, 128), 1)
    diagonal = jnp.where((lane & 63) == iota((FP, 128), 0), qp_ref[...], 0.0)
    for t in range(tiles):
        j = (step * tiles + t) * 2
        s0, s1 = slot_ref[j], slot_ref[j + 1]
        a = got_ref[s0 >> 1].astype(F32)
        b = got_ref[s1 >> 1].astype(F32)
        a = pltpu.roll(a, (s0 & 1) * 64, 1)
        b = pltpu.roll(b, (1 - (s1 & 1)) * 64, 1)
        tile = jnp.where(lane < FP, a, b)
        tile = tile + jnp.where(j + (lane >> 6) == first, diagonal, 0.0)
        out_ref[:, t * 128 : t * 128 + 128] = tile.astype(BF16)


def shift(x, axis, size, by):
    return lax.ppermute(x, axis, [(i, (i + by) % size) for i in range(size)])


def body(coarse_kernel, row_intersection, col_intersection, row_nearest, col_nearest, qp_energy):
    y, z, core, band = (lax.axis_index(a) for a in ("y", "z", "core", "band"))
    near = [coarse_kernel] + [shift(coarse_kernel, "band", NB, d) for d in range(1, NB)]
    pick = (band - row_nearest) % NB
    c, v = row_intersection[0, 0], row_intersection[1, 0]
    row_coef = (c[:, None, :, None] * v[None, :, None, :]).reshape(FP, CP).astype(BF16)

    smem = pl.BlockSpec(memory_space=pltpu.SMEM)
    limit = pltpu.CompilerParams(vmem_limit_bytes=48 * 2**20)
    request, slot = pl.pallas_call(
        request_kernel,
        in_specs=[smem] + whole(4),
        out_specs=whole(2),
        out_shape=[
            jax.ShapeDtypeStruct((GROUP, CAP, NZ, 768), BF16),
            jax.ShapeDtypeStruct((1, FC), jnp.int32),
        ],
        compiler_params=limit,
        name="request",
    )(
        z[None],
        col_nearest[None, :],
        col_nearest[:, None],
        col_intersection[0].reshape(FC, 96),
        col_intersection[1].reshape(FC, 96),
    )
    request = lax.all_to_all(request, ("y", "core"), 0, 0, tiled=True)
    lanes = GROUP * CAP * FP
    u, v, local = pl.pallas_call(
        expand_kernel,
        in_specs=whole(1),
        out_specs=whole(3),
        out_shape=[
            jax.ShapeDtypeStruct((GROUP, NBC * NZ, 128), F32),
            jax.ShapeDtypeStruct((GROUP, NBC * NZ, 128), F32),
            jax.ShapeDtypeStruct((NZ, lanes), F32),
        ],
        compiler_params=limit,
        name="expand",
    )(request)

    own = pl.pallas_call(
        strip_kernel,
        in_specs=[smem] + whole(5),
        out_specs=whole(1)[0],
        out_shape=jax.ShapeDtypeStruct((2, CP, 128), BF16),
        compiler_params=limit,
        name="strip",
    )(pick, *near, row_coef)

    chains = []
    for sign in (1, -1):
        one = shift(own, "z", NZ, sign)
        two = shift(jnp.concatenate([own, one]), "z", NZ, 2 * sign)
        four = shift(two, "z", NZ, 2 * sign)
        half = four[2:3] if sign == 1 else four[3:4]
        six = shift(jnp.concatenate([two[2:], four[:2], half]), "z", NZ, 3 * sign)
        chains.append((one, two, four, six))
    (p1, p2, p4, p6), (n1, n2, n4, n6) = chains
    strips = [own, p1, n1, p2, n2, p4, n4, p6, n6]
    places = [(0, ((0, 0), (0, 1))), (1, ((1, 0), (1, 1))), (2, ((2, 0), (2, 1)))]
    pos = 3
    for a in range(3, 9):
        for b in range(2):
            places.append((pos, ((a, 2 * b), (a, 2 * b + 1))))
            pos += 1
    places.append((15, ((7, 4), (8, 4))))

    def kernel(*refs):
        result_kernel(places, *refs)

    results = pl.pallas_call(
        kernel,
        in_specs=whole(3 + len(strips)),
        out_specs=whole(1)[0],
        out_shape=jax.ShapeDtypeStruct((GROUP, NZ, FP, 128), BF16),
        compiler_params=limit,
        name="result",
    )(u, v, local, *strips)
    got = lax.all_to_all(results, ("y", "core"), 0, 0, tiled=True)

    first = jnp.where((y == 0) & (z == 0) & (core == 0), band, -1)
    steps = 8
    columns = FC * FP
    return pl.pallas_call(
        assemble_kernel,
        grid=(steps,),
        in_specs=[
            smem,
            smem,
            pl.BlockSpec((GROUP * NZ, FP, 128), lambda i: (0, 0, 0)),
            pl.BlockSpec((FP, 1), lambda i: (0, 0)),
        ],
        out_specs=pl.BlockSpec((FP, columns // steps), lambda i: (0, i)),
        out_shape=jax.ShapeDtypeStruct((FP, columns), BF16),
        compiler_params=limit,
        name="assemble",
    )(slot.reshape(FC), first[None], got.reshape(GROUP * NZ, FP, 128), qp_energy[:, None])


def solution(mesh):
    fine = Mesh(mesh.devices.reshape(NY, NZ, NC, NB), ("y", "z", "core", "band"))
    kcol = ("y", "z", "core")
    return jax.shard_map(
        body,
        mesh=fine,
        in_specs=(
            P("band", kcol),
            P(None, "band", None, None),
            P(None, kcol, None, None),
            P("band"),
            P(kcol),
            P("band"),
        ),
        out_specs=P("band", kcol),
        check_vma=False,
    )
```

```python
import functools

import jax
import jax.numpy as jnp
from jax import lax
from jax.experimental import pallas as pl
from jax.experimental.pallas import tpu as pltpu
from jax.sharding import Mesh
from jax.sharding import PartitionSpec as P

NBF = 8
NBC = 12
FP = NBF * NBF
CP = NBC * NBC
RC = 4
NY, NZ, NC, NB = 4, 16, 2, 4
GROUP = NY * NC
FC = 144
HELD = 4
CAP = 2
PARTS = ((0, 5), (5, 11), (11, 16))
HALF = NZ // 2
COSTS = (10, 20, 4)
F32 = jnp.float32
BF16 = jnp.bfloat16


def iota(shape, dim):
    return lax.broadcasted_iota(jnp.int32, shape, dim)


def dot(a, b, dims=((1,), (0,))):
    return lax.dot_general(a, b, (dims, ((), ())), preferred_element_type=F32)


def whole(n):
    return [pl.BlockSpec(memory_space=pltpu.VMEM)] * n


def strip_kernel(pick_ref, k0, k1, k2, k3, coef_ref, out_ref):
    pick = pick_ref[0]
    rows = jnp.where(pick == 0, k0[...], k1[...])
    rows = jnp.where(pick == 2, k2[...], rows)
    rows = jnp.where(pick == 3, k3[...], rows)
    strip = dot(rows, coef_ref[...], ((0,), (1,))).astype(BF16)
    to = iota((CP, CP), 0)
    low = (to >> 3) * NBC + (to & 7)
    high = ((to - 96) >> 2) * NBC + 8 + (to & 3)
    order = (jnp.where(to < 96, low, high) == iota((CP, CP), 1)).astype(BF16)
    for pair in range(2):
        at = pair * 2 * CP
        both = jnp.concatenate([strip[at : at + CP], strip[at + CP : at + 2 * CP]], axis=1)
        out_ref[pair] = dot(order, both).astype(BF16)


def request_kernel(z_ref, row_ref, conduction_ref, valence_ref, out_ref, block_ref):
    z = z_ref[0]
    near = row_ref[...]
    holder = near >> 2
    square = (FC, FC)
    here = iota(square, 0) == iota(square, 1)
    column = jnp.sum(jnp.where(here, near, 0), axis=1, keepdims=True)
    earlier = ((column >> 2) == holder) & (iota(square, 0) < iota(square, 1))
    rank = jnp.sum(earlier.astype(jnp.int32), axis=0, keepdims=True)
    rel = ((holder >> 1) - z) & (NZ - 1)
    far = jnp.minimum(rel, NZ - rel)
    core = holder & 1
    server = jnp.where((far & 7) == 0, core, (rel < 8).astype(jnp.int32))
    pos = jnp.where((far & 7) == 0, (far >> 3) * 15, 2 * far - 1 + (core ^ server))
    group = (holder >> 5) * NC + server
    slot = (group * NZ + pos) * CAP + rank
    block = jnp.zeros_like(pos)
    for lo, hi in PARTS:
        block = jnp.where((pos >= lo) & (pos < hi), lo * GROUP + group * (hi - lo) + pos - lo, block)
    block_ref[...] = block * CAP + rank
    lanes = 12 * 64
    source = iota((96, lanes), 0)
    lane = iota((96, lanes), 1)
    i, inner = lane >> 6, lane & 63
    spot = (inner & 7) * NBC + i
    table = jnp.zeros((FC, lanes), F32)
    for t, ref in enumerate((conduction_ref, valence_ref)):
        rest = ref[...]
        for s in range(3):
            term = rest.astype(BF16)
            rest = rest - term.astype(F32)
            place = ((source == spot) & ((inner >> 3) == s * 2 + t)).astype(BF16)
            table = table + dot(term, place)
    local = (column & 3).astype(F32)
    table = jnp.where((iota((FC, lanes), 1) & 63) == 48, local, table).astype(BF16)
    row = iota((GROUP * NZ, FC), 0) * CAP
    for r in range(CAP):
        one = (slot == row + r).astype(BF16)
        out_ref[:, r] = dot(one, table).astype(BF16).reshape(GROUP, NZ, lanes)


def expand_kernel(x_ref, u0_ref, v0_ref, u1_ref, v1_ref, local_ref):
    k = iota((256, 512), 0)
    n = iota((256, 512), 1)
    inner = k & 63
    want = jnp.where((n & 128) == 0, (n >> 3) & 7, n & 7)
    same = ((k >> 7) == ((n >> 6) & 1)) & (((k >> 6) & 1) == (n >> 8))
    same = same & (inner < 48) & (((inner >> 3) & 1) == ((n >> 7) & 1)) & ((inner & 7) == want)
    spread = same.astype(BF16)
    k = iota((256, 128), 0)
    n = iota((256, 128), 1)
    spread_local = (((k & 127) == 48) & ((k >> 7) == (n >> 6))).astype(BF16)
    for d in range(GROUP):
        lanes = pl.ds(d * 128, 128)
        for m in range(6):
            at = pl.ds(m * 128, 128)
            x = jnp.concatenate([x_ref[d, 0, :, at], x_ref[d, 1, :, at]], axis=1)
            y = dot(x, spread)
            for half in range(2):
                rows = pl.ds((m * 2 + half) * HALF, HALF)
                for n, (u_ref, v_ref) in enumerate(((u0_ref, v0_ref), (u1_ref, v1_ref))):
                    part = y[n * HALF : (n + 1) * HALF, half * 256 : half * 256 + 256]
                    u_ref[d, rows] = part[:, :128]
                    v_ref[d, rows] = part[:, 128:]
            if m == 0:
                local_ref[:, lanes] = dot(x, spread_local)


def coefficients(u_ref, v_ref, d, pos):
    u = [jnp.broadcast_to(u_ref[d, pl.ds(i * HALF + pos, 1)], (8, 128)) for i in range(NBC)]
    v_low = v_ref[d, pl.ds(pos, 8, stride=HALF)]
    v_high = v_ref[d, pl.ds(8 * HALF + pos, 4, stride=HALF)]
    v_high = jnp.concatenate([v_high, v_high], axis=0)
    first = iota((8, 128), 0) < 4
    parts = [v_low * u[i] for i in range(NBC)]
    parts += [v_high * jnp.where(first, u[i], u[i + 1]) for i in range(0, NBC, 2)]
    return jnp.concatenate(parts, axis=0).astype(BF16)


def result_kernel(places, halves, local_ref, *refs):
    factors = {h: refs[2 * n : 2 * n + 2] for n, h in enumerate(halves)}
    strips, out_ref = refs[2 * len(halves) : -1], refs[-1]
    for at, (pos, pairs) in enumerate(places):
        blocks = [strips[a][b] for a, b in pairs]
        u_ref, v_ref = factors[pos // HALF]
        for chunk in range(4):
            lanes = pl.ds(chunk * 256, 256)
            coef = jnp.concatenate([coefficients(u_ref, v_ref, 2 * chunk + d, pos % HALF) for d in range(2)], axis=1)
            low = dot(blocks[0], coef, ((0,), (0,)))
            high = dot(blocks[1], coef, ((0,), (0,)))
            local = local_ref[pl.ds(pos, 1), lanes]
            res = jnp.where(local == 0, low[:FP], low[FP:])
            res = jnp.where(local == 2, high[:FP], res)
            res = jnp.where(local == 3, high[FP:], res).astype(BF16)
            for half in range(2):
                out_ref[chunk * 2 + half, at] = res[:, half * 128 : half * 128 + 128]


def assemble_kernel(block_ref, where_ref, *refs):
    parts, (qp_ref, out_ref, got_ref, sems) = refs[: len(PARTS)], refs[len(PARTS) :]
    step = pl.program_id(0)

    @pl.when(step == 0)
    def _():
        copies = []
        for n, (lo, hi) in enumerate(PARTS):
            at = pl.ds(lo * GROUP, (hi - lo) * GROUP)
            copies.append(pltpu.make_async_copy(parts[n], got_ref.at[at], sems.at[n]))
            copies[-1].start()
        for copy in copies:
            copy.wait()

    tiles = out_ref.shape[1] // 128
    first = where_ref[0]
    lane = iota((FP, 128), 1)
    diagonal = jnp.where((lane & 63) == iota((FP, 128), 0), qp_ref[...], 0.0)
    for t in range(tiles):
        j = (step * tiles + t) * 2
        s0, s1 = block_ref[j], block_ref[j + 1]
        a = got_ref[s0 >> 1].astype(F32)
        b = got_ref[s1 >> 1].astype(F32)
        a = pltpu.roll(a, (s0 & 1) * 64, 1)
        b = pltpu.roll(b, (1 - (s1 & 1)) * 64, 1)
        out_ref[:, t * 128 : t * 128 + 128] = jnp.where(lane < FP, a, b).astype(BF16)

    @pl.when((step == 0) & (first >= 0))
    def _():
        for t in range(2):
            at = slice(t * 128, t * 128 + 128)
            add = jnp.where(2 * t + (lane >> 6) == first, diagonal, 0.0)
            out_ref[:, at] = (out_ref[:, at].astype(F32) + add).astype(BF16)


def shift(x, axis, size, by):
    return lax.ppermute(x, axis, [(i, (i + by) % size) for i in range(size)])


def along(x, by):
    pairs = [(z * NC + c, (z + (by if c == 0 else -by)) % NZ * NC + c) for z in range(NZ) for c in range(NC)]
    return lax.ppermute(x, ("z", "core"), pairs)


def body(coarse_kernel, row_intersection, col_intersection, row_nearest, col_nearest, qp_energy):
    y, z, core, band = (lax.axis_index(a) for a in ("y", "z", "core", "band"))
    near = [coarse_kernel] + [shift(coarse_kernel, "band", NB, d) for d in range(1, NB)]
    pick = (band - row_nearest) % NB
    c, v = row_intersection[0, 0], row_intersection[1, 0]
    row_coef = (c[:, None, :, None] * v[None, :, None, :]).reshape(FP, CP).astype(BF16)

    smem = pl.BlockSpec(memory_space=pltpu.SMEM)
    limit = pltpu.CompilerParams(vmem_limit_bytes=16 * 2**20)
    request, block = pl.pallas_call(
        request_kernel,
        in_specs=[smem] + whole(3),
        out_specs=whole(2),
        out_shape=[
            jax.ShapeDtypeStruct((GROUP, CAP, NZ, 768), BF16),
            jax.ShapeDtypeStruct((1, FC), jnp.int32),
        ],
        compiler_params=limit,
        name="request",
    )(
        z[None],
        col_nearest[None, :],
        col_intersection[0].reshape(FC, 96),
        col_intersection[1].reshape(FC, 96),
    )
    request, *near = lax.optimization_barrier((request, *near))
    request = lax.all_to_all(request, ("y", "core"), 0, 0, tiled=True)
    lanes = GROUP * CAP * FP
    *factors, local = pl.pallas_call(
        expand_kernel,
        in_specs=whole(1),
        out_specs=whole(5),
        out_shape=[
            *[jax.ShapeDtypeStruct((GROUP, NBC * HALF, 128), F32)] * 4,
            jax.ShapeDtypeStruct((NZ, lanes), F32),
        ],
        compiler_params=limit,
        name="expand",
    )(request)

    own = pl.pallas_call(
        strip_kernel,
        in_specs=[smem] + whole(5),
        out_specs=whole(1)[0],
        out_shape=jax.ShapeDtypeStruct((2, CP, 128), BF16),
        compiler_params=limit,
        name="strip",
    )(pick, *near, row_coef)

    own = jnp.concatenate([own, shift(own, "core", NC, 1)])
    one = along(own, 1)
    two = along(jnp.concatenate([own, one]), 2)
    four = along(two, 2)
    six = along(four, 2)
    eight = along(six[4:6], 1)
    strips = [own, one, two, four, six, eight]
    places = [(0, ((0, 0), (0, 1)))]
    for a, blocks in ((1, 2), (2, 4), (3, 4), (4, 4), (5, 1)):
        places += [(len(places) + b, ((a, 2 * b), (a, 2 * b + 1))) for b in range(blocks)]

    got = []
    for lo, hi in PARTS:
        used = sorted({a for _, pairs in places[lo:hi] for a, _ in pairs})
        halves = sorted({pos // HALF for pos in range(lo, hi)})
        mine = [(pos, tuple((used.index(a), b) for a, b in pairs)) for pos, pairs in places[lo:hi]]
        if got:
            local, last = lax.optimization_barrier((local, last))
        results = pl.pallas_call(
            functools.partial(result_kernel, mine, halves),
            in_specs=whole(1 + 2 * len(halves) + len(used)),
            out_specs=whole(1)[0],
            out_shape=jax.ShapeDtypeStruct((GROUP, hi - lo, FP, 128), BF16),
            compiler_params=limit,
            cost_estimate=pl.CostEstimate(flops=COSTS[len(got)] * 10**9, bytes_accessed=10**6, transcendentals=0),
            name="result",
        )(local, *[f for h in halves for f in factors[2 * h : 2 * h + 2]], *[strips[a] for a in used])
        last = results
        if got:
            results, got[-1] = lax.optimization_barrier((results, got[-1]))
        got.append(lax.all_to_all(results, ("y", "core"), 0, 0, tiled=True).reshape(-1, FP, 128))

    first = jnp.where((y == 0) & (z == 0) & (core == 0), band, -1)
    steps = 4
    columns = FC * FP
    return pl.pallas_call(
        assemble_kernel,
        grid=(steps,),
        in_specs=[
            smem,
            smem,
            *[pl.BlockSpec(memory_space=pl.ANY)] * len(got),
            pl.BlockSpec((FP, 1), lambda i: (0, 0)),
        ],
        out_specs=pl.BlockSpec((FP, columns // steps), lambda i: (0, i)),
        out_shape=jax.ShapeDtypeStruct((FP, columns), BF16),
        scratch_shapes=[pltpu.VMEM((GROUP * NZ, FP, 128), BF16), pltpu.SemaphoreType.DMA((len(got),))],
        compiler_params=limit,
        name="assemble",
    )(block.reshape(FC), first[None], *got, qp_energy[:, None])


def solution(mesh):
    fine = Mesh(mesh.devices.reshape(NY, NZ, NC, NB), ("y", "z", "core", "band"))
    kcol = ("y", "z", "core")
    return jax.shard_map(
        body,
        mesh=fine,
        in_specs=(
            P("band", kcol),
            P(None, "band", None, None),
            P(None, kcol, None, None),
            P("band"),
            P(kcol),
            P("band"),
        ),
        out_specs=P("band", kcol),
        check_vma=False,
    )
```

```python
import functools

import jax
import jax.numpy as jnp
from jax import lax
from jax.experimental import pallas as pl
from jax.experimental.pallas import tpu as pltpu
from jax.sharding import Mesh
from jax.sharding import PartitionSpec as P

NBF = 8
NBC = 12
FP = NBF * NBF
CP = NBC * NBC
RC = 4
NY, NZ, NC, NB = 4, 16, 2, 4
GROUP = NY * NC
FC = 144
HELD = 4
CAP = 2
PARTS = ((0, 6), (6, 11), (11, 16))
RANGES = (((0, 3), (3, 6)), ((6, 11),), ((11, 16),))
HALF = NZ // 2
COSTS = {0: 0, 3: 10, 6: 20, 11: 4}
F32 = jnp.float32
BF16 = jnp.bfloat16


def iota(shape, dim):
    return lax.broadcasted_iota(jnp.int32, shape, dim)


def dot(a, b, dims=((1,), (0,))):
    return lax.dot_general(a, b, (dims, ((), ())), preferred_element_type=F32)


def whole(n):
    return [pl.BlockSpec(memory_space=pltpu.VMEM)] * n


def strip_kernel(pick_ref, k0, k2, k1, k3, coef_ref, out_ref):
    pick = pick_ref[0]
    rows = jnp.where(pick == 0, k0[...], k1[...])
    rows = jnp.where(pick == 2, k2[...], rows)
    rows = jnp.where(pick == 3, k3[...], rows)
    strip = dot(rows, coef_ref[...], ((0,), (1,))).astype(BF16)
    to = iota((CP, CP), 0)
    low = (to >> 3) * NBC + (to & 7)
    high = ((to - 96) >> 2) * NBC + 8 + (to & 3)
    order = (jnp.where(to < 96, low, high) == iota((CP, CP), 1)).astype(BF16)
    for pair in range(2):
        at = pair * 2 * CP
        both = jnp.concatenate([strip[at : at + CP], strip[at + CP : at + 2 * CP]], axis=1)
        out_ref[pair] = dot(order, both).astype(BF16)


def request_kernel(z_ref, row_ref, conduction_ref, valence_ref, out_ref, block_ref):
    z = z_ref[0]
    near = row_ref[...]
    holder = near >> 2
    square = (FC, FC)
    here = iota(square, 0) == iota(square, 1)
    column = jnp.sum(jnp.where(here, near, 0), axis=1, keepdims=True)
    earlier = ((column >> 2) == holder) & (iota(square, 0) < iota(square, 1))
    rank = jnp.sum(earlier.astype(jnp.int32), axis=0, keepdims=True)
    rel = ((holder >> 1) - z) & (NZ - 1)
    far = jnp.minimum(rel, NZ - rel)
    core = holder & 1
    server = jnp.where((far & 7) == 0, core, (rel < 8).astype(jnp.int32))
    pos = jnp.where((far & 7) == 0, (far >> 3) * 15, 2 * far - 1 + (core ^ server))
    group = (holder >> 5) * NC + server
    slot = (group * NZ + pos) * CAP + rank
    block = jnp.zeros_like(pos)
    for lo, hi in PARTS:
        block = jnp.where((pos >= lo) & (pos < hi), lo * GROUP + group * (hi - lo) + pos - lo, block)
    block_ref[...] = block * CAP + rank
    lanes = 12 * 64
    source = iota((96, lanes), 0)
    lane = iota((96, lanes), 1)
    i, inner = lane >> 6, lane & 63
    spot = (inner & 7) * NBC + i
    table = jnp.zeros((FC, lanes), F32)
    for t, ref in enumerate((conduction_ref, valence_ref)):
        rest = ref[...]
        for s in range(3):
            term = rest.astype(BF16)
            rest = rest - term.astype(F32)
            place = ((source == spot) & ((inner >> 3) == s * 2 + t)).astype(BF16)
            table = table + dot(term, place)
    local = (column & 3).astype(F32)
    table = jnp.where((iota((FC, lanes), 1) & 63) == 48, local, table).astype(BF16)
    row = iota((GROUP * NZ, FC), 0) * CAP
    for r in range(CAP):
        one = (slot == row + r).astype(BF16)
        out_ref[:, r] = dot(one, table).astype(BF16).reshape(GROUP, NZ, lanes)


def expand_kernel(x_ref, u0_ref, v0_ref, u1_ref, v1_ref, local_ref):
    k = iota((256, 512), 0)
    n = iota((256, 512), 1)
    inner = k & 63
    want = jnp.where((n & 128) == 0, (n >> 3) & 7, n & 7)
    same = ((k >> 7) == ((n >> 6) & 1)) & (((k >> 6) & 1) == (n >> 8))
    same = same & (inner < 48) & (((inner >> 3) & 1) == ((n >> 7) & 1)) & ((inner & 7) == want)
    spread = same.astype(BF16)
    k = iota((256, 128), 0)
    n = iota((256, 128), 1)
    spread_local = (((k & 127) == 48) & ((k >> 7) == (n >> 6))).astype(BF16)
    for d in range(GROUP):
        lanes = pl.ds(d * 128, 128)
        for m in range(6):
            at = pl.ds(m * 128, 128)
            x = jnp.concatenate([x_ref[d, 0, :, at], x_ref[d, 1, :, at]], axis=1)
            y = dot(x, spread)
            for half in range(2):
                rows = pl.ds((m * 2 + half) * HALF, HALF)
                for n, (u_ref, v_ref) in enumerate(((u0_ref, v0_ref), (u1_ref, v1_ref))):
                    part = y[n * HALF : (n + 1) * HALF, half * 256 : half * 256 + 256]
                    u_ref[d, rows] = part[:, :128]
                    v_ref[d, rows] = part[:, 128:]
            if m == 0:
                local_ref[:, lanes] = dot(x, spread_local)


def coefficients(u_ref, v_ref, d, pos):
    u = [jnp.broadcast_to(u_ref[d, pl.ds(i * HALF + pos, 1)], (8, 128)) for i in range(NBC)]
    v_low = v_ref[d, pl.ds(pos, 8, stride=HALF)]
    v_high = v_ref[d, pl.ds(8 * HALF + pos, 4, stride=HALF)]
    v_high = jnp.concatenate([v_high, v_high], axis=0)
    first = iota((8, 128), 0) < 4
    parts = [v_low * u[i] for i in range(NBC)]
    parts += [v_high * jnp.where(first, u[i], u[i + 1]) for i in range(0, NBC, 2)]
    return jnp.concatenate(parts, axis=0).astype(BF16)


def result_kernel(places, halves, offset, local_ref, *refs):
    factors = {h: refs[2 * n : 2 * n + 2] for n, h in enumerate(halves)}
    strips, (out_ref, kept_ref, sems) = refs[2 * len(halves) : -3], refs[-3:]
    copies = []
    for at, (pos, pairs) in enumerate(places):
        blocks = [strips[a][b] for a, b in pairs]
        u_ref, v_ref = factors[pos // HALF]
        for chunk in range(4):
            lanes = pl.ds(chunk * 256, 256)
            coef = jnp.concatenate([coefficients(u_ref, v_ref, 2 * chunk + d, pos % HALF) for d in range(2)], axis=1)
            low = dot(blocks[0], coef, ((0,), (0,)))
            high = dot(blocks[1], coef, ((0,), (0,)))
            local = local_ref[pl.ds(pos, 1), lanes]
            res = jnp.where(local == 0, low[:FP], low[FP:])
            res = jnp.where(local == 2, high[:FP], res)
            res = jnp.where(local == 3, high[FP:], res).astype(BF16)
            for half in range(2):
                kept_ref[at, chunk * 2 + half] = res[:, half * 128 : half * 128 + 128]
        copies.append(pltpu.make_async_copy(kept_ref.at[at], out_ref.at[:, offset + at], sems.at[at]))
        copies[-1].start()
    for copy in copies:
        copy.wait()


def assemble_kernel(block_ref, where_ref, *refs):
    parts, (qp_ref, out_ref, got_ref, full_ref, in_sems, out_sems) = refs[: len(PARTS)], refs[len(PARTS) :]
    copies = []
    for n, (lo, hi) in enumerate(PARTS):
        at = pl.ds(lo * GROUP, (hi - lo) * GROUP)
        copies.append(pltpu.make_async_copy(parts[n], got_ref.at[at], in_sems.at[n]))
        copies[-1].start()
    for copy in copies:
        copy.wait()
    first = where_ref[0]
    lane = iota((FP, 128), 1)
    tiles = FC // 2
    chunks = out_sems.shape[0]
    copies = []
    for chunk in range(chunks):
        for t in range(chunk * tiles // chunks, (chunk + 1) * tiles // chunks):
            s0, s1 = block_ref[2 * t], block_ref[2 * t + 1]
            a = pltpu.roll(got_ref[s0 >> 1], (s0 & 1) * 64, 1)
            b = pltpu.roll(got_ref[s1 >> 1], (1 - (s1 & 1)) * 64, 1)
            full_ref[:, t * 128 : t * 128 + 128] = jnp.where(lane < FP, a, b)
        if chunk == 0:

            @pl.when(first >= 0)
            def _():
                diagonal = jnp.where((lane & 63) == iota((FP, 128), 0), qp_ref[...], 0.0)
                for t in range(2):
                    at = slice(t * 128, t * 128 + 128)
                    add = jnp.where(2 * t + (lane >> 6) == first, diagonal, 0.0)
                    full_ref[:, at] = (full_ref[:, at].astype(F32) + add).astype(BF16)

        at = pl.ds(chunk * tiles // chunks * 128, tiles // chunks * 128)
        copies.append(pltpu.make_async_copy(full_ref.at[:, at], out_ref.at[:, at], out_sems.at[chunk]))
        copies[-1].start()
    for copy in copies:
        copy.wait()


def shift(x, axis, size, by):
    return lax.ppermute(x, axis, [(i, (i + by) % size) for i in range(size)])


def along(x, by):
    pairs = [(z * NC + c, (z + (by if c == 0 else -by)) % NZ * NC + c) for z in range(NZ) for c in range(NC)]
    return lax.ppermute(x, ("z", "core"), pairs)


def body(coarse_kernel, row_intersection, col_intersection, row_nearest, col_nearest, qp_energy):
    y, z, core, band = (lax.axis_index(a) for a in ("y", "z", "core", "band"))
    near = [coarse_kernel] + [shift(coarse_kernel, "band", NB, d) for d in (2, 1, 3)]
    pick = (band - row_nearest) % NB
    c, v = row_intersection[0, 0], row_intersection[1, 0]
    row_coef = (c[:, None, :, None] * v[None, :, None, :]).reshape(FP, CP).astype(BF16)

    smem = pl.BlockSpec(memory_space=pltpu.SMEM)
    limit = pltpu.CompilerParams(vmem_limit_bytes=16 * 2**20)
    request, block = pl.pallas_call(
        request_kernel,
        in_specs=[smem] + whole(3),
        out_specs=whole(2),
        out_shape=[
            jax.ShapeDtypeStruct((GROUP, CAP, NZ, 768), BF16),
            jax.ShapeDtypeStruct((1, FC), jnp.int32),
        ],
        compiler_params=limit,
        name="request",
    )(
        z[None],
        col_nearest[None, :],
        col_intersection[0].reshape(FC, 96),
        col_intersection[1].reshape(FC, 96),
    )
    request, *near = lax.optimization_barrier((request, *near))
    request = lax.all_to_all(request, ("y", "core"), 0, 0, tiled=True)
    lanes = GROUP * CAP * FP
    *factors, local = pl.pallas_call(
        expand_kernel,
        in_specs=whole(1),
        out_specs=whole(5),
        out_shape=[
            *[jax.ShapeDtypeStruct((GROUP, NBC * HALF, 128), F32)] * 4,
            jax.ShapeDtypeStruct((NZ, lanes), F32),
        ],
        compiler_params=limit,
        name="expand",
    )(request)

    own = pl.pallas_call(
        strip_kernel,
        in_specs=[smem] + whole(5),
        out_specs=whole(1)[0],
        out_shape=jax.ShapeDtypeStruct((2, CP, 128), BF16),
        compiler_params=limit,
        cost_estimate=pl.CostEstimate(flops=0, bytes_accessed=0, transcendentals=0),
        name="strip",
    )(pick, *near, row_coef)

    own = jnp.concatenate([own, shift(own, "core", NC, 1)])
    one = along(own, 1)
    two = along(jnp.concatenate([own, one]), 2)
    four = along(two, 2)
    six = along(four, 2)
    eight = along(six[4:6], 1)
    strips = [own, one, two, four, six, eight]
    places = [(0, ((0, 0), (0, 1)))]
    for a, blocks in ((1, 2), (2, 4), (3, 4), (4, 4), (5, 1)):
        places += [(len(places) + b, ((a, 2 * b), (a, 2 * b + 1))) for b in range(blocks)]

    anywhere = pl.BlockSpec(memory_space=pl.ANY)
    got = []
    for n, (low, high) in enumerate(PARTS):
        results = []
        for lo, hi in RANGES[n]:
            used = sorted({a for _, pairs in places[lo:hi] for a, _ in pairs})
            halves = sorted({pos // HALF for pos in range(lo, hi)})
            mine = [(pos, tuple((used.index(a), b) for a, b in pairs)) for pos, pairs in places[lo:hi]]
            operands = [local, *[f for h in halves for f in factors[2 * h : 2 * h + 2]], *[strips[a] for a in used]]
            result = pl.pallas_call(
                functools.partial(result_kernel, mine, halves, lo - low),
                in_specs=whole(len(operands)) + [anywhere] * len(results),
                out_specs=anywhere,
                out_shape=jax.ShapeDtypeStruct((GROUP, high - low, FP, 128), BF16),
                input_output_aliases={len(operands): 0} if results else {},
                scratch_shapes=[pltpu.VMEM((hi - lo, GROUP, FP, 128), BF16), pltpu.SemaphoreType.DMA((hi - lo,))],
                compiler_params=limit,
                cost_estimate=pl.CostEstimate(flops=COSTS[lo] * 10**9, bytes_accessed=10**6, transcendentals=0),
                name="result",
            )(*operands, *results)
            results = [result]
            local, result = lax.optimization_barrier((local, result))
            results = [result]
        if got:
            result, got[-1] = lax.optimization_barrier((result, got[-1]))
        got.append(lax.all_to_all(result, ("y", "core"), 0, 0, tiled=True).reshape(-1, FP, 128))

    first = jnp.where((y == 0) & (z == 0) & (core == 0), band, -1)
    return pl.pallas_call(
        assemble_kernel,
        in_specs=[smem, smem, *[anywhere] * len(got), *whole(1)],
        out_specs=anywhere,
        out_shape=jax.ShapeDtypeStruct((FP, FC * FP), BF16),
        scratch_shapes=[
            pltpu.VMEM((GROUP * NZ, FP, 128), BF16),
            pltpu.VMEM((FP, FC * FP), BF16),
            pltpu.SemaphoreType.DMA((len(got),)),
            pltpu.SemaphoreType.DMA((12,)),
        ],
        compiler_params=limit,
        name="assemble",
    )(block.reshape(FC), first[None], *got, qp_energy[:, None])


def solution(mesh):
    fine = Mesh(mesh.devices.reshape(NY, NZ, NC, NB), ("y", "z", "core", "band"))
    kcol = ("y", "z", "core")
    return jax.shard_map(
        body,
        mesh=fine,
        in_specs=(
            P("band", kcol),
            P(None, "band", None, None),
            P(None, kcol, None, None),
            P("band"),
            P(kcol),
            P("band"),
        ),
        out_specs=P("band", kcol),
        check_vma=False,
    )
```

```python
import functools

import jax
import jax.numpy as jnp
from jax import lax
from jax.experimental import pallas as pl
from jax.experimental.pallas import tpu as pltpu
from jax.sharding import Mesh
from jax.sharding import PartitionSpec as P

NBF = 8
NBC = 12
FP = NBF * NBF
CP = NBC * NBC
RC = 4
NY, NZ, NC, NB = 4, 16, 2, 4
GROUP = NY * NC
FC = 144
HELD = 4
CAP = 2
PARTS = ((0, 6), (6, 11), (11, 16))
RANGES = (((0, 3), (3, 6)), ((6, 11),), ((11, 15), (15, 16)))
HALF = NZ // 2
COSTS = {0: 0, 3: 10, 6: 20, 11: 4, 15: 0}
F32 = jnp.float32
BF16 = jnp.bfloat16


def iota(shape, dim):
    return lax.broadcasted_iota(jnp.int32, shape, dim)


def dot(a, b, dims=((1,), (0,))):
    return lax.dot_general(a, b, (dims, ((), ())), preferred_element_type=F32)


def whole(n):
    return [pl.BlockSpec(memory_space=pltpu.VMEM)] * n


def strip_kernel(pick_ref, k0, k2, k1, k3, coef_ref, out_ref):
    pick = pick_ref[0]
    rows = jnp.where(pick == 0, k0[...], k1[...])
    rows = jnp.where(pick == 2, k2[...], rows)
    rows = jnp.where(pick == 3, k3[...], rows)
    strip = dot(rows, coef_ref[...], ((0,), (1,))).astype(BF16)
    to = iota((CP, CP), 0)
    low = (to >> 3) * NBC + (to & 7)
    high = ((to - 96) >> 2) * NBC + 8 + (to & 3)
    order = (jnp.where(to < 96, low, high) == iota((CP, CP), 1)).astype(BF16)
    for pair in range(2):
        at = pair * 2 * CP
        both = jnp.concatenate([strip[at : at + CP], strip[at + CP : at + 2 * CP]], axis=1)
        out_ref[pair] = dot(order, both).astype(BF16)


def request_kernel(z_ref, row_ref, conduction_ref, valence_ref, out_ref, block_ref):
    z = z_ref[0]
    near = row_ref[...]
    holder = near >> 2
    square = (FC, FC)
    here = iota(square, 0) == iota(square, 1)
    column = jnp.sum(jnp.where(here, near, 0), axis=1, keepdims=True)
    earlier = ((column >> 2) == holder) & (iota(square, 0) < iota(square, 1))
    rank = jnp.sum(earlier.astype(jnp.int32), axis=0, keepdims=True)
    rel = ((holder >> 1) - z) & (NZ - 1)
    far = jnp.minimum(rel, NZ - rel)
    core = holder & 1
    server = jnp.where((far & 7) == 0, core, (rel < 8).astype(jnp.int32))
    pos = jnp.where((far & 7) == 0, (far >> 3) * 15, 2 * far - 1 + (core ^ server))
    group = (holder >> 5) * NC + server
    slot = (group * NZ + pos) * CAP + rank
    block = jnp.zeros_like(pos)
    for lo, hi in PARTS:
        block = jnp.where((pos >= lo) & (pos < hi), lo * GROUP + group * (hi - lo) + pos - lo, block)
    block_ref[...] = block * CAP + rank
    lanes = 12 * 64
    source = iota((96, lanes), 0)
    lane = iota((96, lanes), 1)
    i, inner = lane >> 6, lane & 63
    spot = (inner & 7) * NBC + i
    table = jnp.zeros((FC, lanes), F32)
    for t, ref in enumerate((conduction_ref, valence_ref)):
        rest = ref[...]
        for s in range(3):
            term = rest.astype(BF16)
            rest = rest - term.astype(F32)
            place = ((source == spot) & ((inner >> 3) == s * 2 + t)).astype(BF16)
            table = table + dot(term, place)
    local = (column & 3).astype(F32)
    table = jnp.where((iota((FC, lanes), 1) & 63) == 48, local, table).astype(BF16)
    row = iota((GROUP * NZ, FC), 0) * CAP
    for r in range(CAP):
        one = (slot == row + r).astype(BF16)
        out_ref[:, r] = dot(one, table).astype(BF16).reshape(GROUP, NZ, lanes)


def expand_kernel(x_ref, u0_ref, v0_ref, u1_ref, v1_ref, local_ref):
    k = iota((256, 512), 0)
    n = iota((256, 512), 1)
    inner = k & 63
    want = jnp.where((n & 128) == 0, (n >> 3) & 7, n & 7)
    same = ((k >> 7) == ((n >> 6) & 1)) & (((k >> 6) & 1) == (n >> 8))
    same = same & (inner < 48) & (((inner >> 3) & 1) == ((n >> 7) & 1)) & ((inner & 7) == want)
    spread = same.astype(BF16)
    k = iota((256, 128), 0)
    n = iota((256, 128), 1)
    spread_local = (((k & 127) == 48) & ((k >> 7) == (n >> 6))).astype(BF16)
    for d in range(GROUP):
        lanes = pl.ds(d * 128, 128)
        for m in range(6):
            at = pl.ds(m * 128, 128)
            x = jnp.concatenate([x_ref[d, 0, :, at], x_ref[d, 1, :, at]], axis=1)
            y = dot(x, spread)
            for half in range(2):
                rows = pl.ds((m * 2 + half) * HALF, HALF)
                for n, (u_ref, v_ref) in enumerate(((u0_ref, v0_ref), (u1_ref, v1_ref))):
                    part = y[n * HALF : (n + 1) * HALF, half * 256 : half * 256 + 256]
                    u_ref[d, rows] = part[:, :128]
                    v_ref[d, rows] = part[:, 128:]
            if m == 0:
                local_ref[:, lanes] = dot(x, spread_local)


def coefficients(u_ref, v_ref, d, pos):
    u = [jnp.broadcast_to(u_ref[d, pl.ds(i * HALF + pos, 1)], (8, 128)) for i in range(NBC)]
    v_low = v_ref[d, pl.ds(pos, 8, stride=HALF)]
    v_high = v_ref[d, pl.ds(8 * HALF + pos, 4, stride=HALF)]
    v_high = jnp.concatenate([v_high, v_high], axis=0)
    first = iota((8, 128), 0) < 4
    parts = [v_low * u[i] for i in range(NBC)]
    parts += [v_high * jnp.where(first, u[i], u[i + 1]) for i in range(0, NBC, 2)]
    return jnp.concatenate(parts, axis=0).astype(BF16)


def result_kernel(places, halves, offset, local_ref, *refs):
    factors = {h: refs[2 * n : 2 * n + 2] for n, h in enumerate(halves)}
    strips, (out_ref, kept_ref, sems) = refs[2 * len(halves) : -3], refs[-3:]
    copies = []
    for at, (pos, pairs) in enumerate(places):
        blocks = [strips[a][b] for a, b in pairs]
        u_ref, v_ref = factors[pos // HALF]
        for chunk in range(4):
            lanes = pl.ds(chunk * 256, 256)
            coef = jnp.concatenate([coefficients(u_ref, v_ref, 2 * chunk + d, pos % HALF) for d in range(2)], axis=1)
            low = dot(blocks[0], coef, ((0,), (0,)))
            high = dot(blocks[1], coef, ((0,), (0,)))
            local = local_ref[pl.ds(pos, 1), lanes]
            res = jnp.where(local == 0, low[:FP], low[FP:])
            res = jnp.where(local == 2, high[:FP], res)
            res = jnp.where(local == 3, high[FP:], res).astype(BF16)
            for half in range(2):
                kept_ref[at, chunk * 2 + half] = res[:, half * 128 : half * 128 + 128]
        copies.append(pltpu.make_async_copy(kept_ref.at[at], out_ref.at[:, offset + at], sems.at[at]))
        copies[-1].start()
    for copy in copies:
        copy.wait()


def assemble_kernel(block_ref, where_ref, *refs):
    parts, (qp_ref, out_ref, got_ref, full_ref, in_sems, out_sems) = refs[: len(PARTS)], refs[len(PARTS) :]
    copies = []
    for n, (lo, hi) in enumerate(PARTS):
        at = pl.ds(lo * GROUP, (hi - lo) * GROUP)
        copies.append(pltpu.make_async_copy(parts[n], got_ref.at[at], in_sems.at[n]))
        copies[-1].start()
    for copy in copies:
        copy.wait()
    first = where_ref[0]
    lane = iota((FP, 128), 1)
    tiles = FC // 2
    chunks = out_sems.shape[0]
    copies = []
    for chunk in range(chunks):
        for t in range(chunk * tiles // chunks, (chunk + 1) * tiles // chunks):
            s0, s1 = block_ref[2 * t], block_ref[2 * t + 1]
            a = pltpu.roll(got_ref[s0 >> 1], (s0 & 1) * 64, 1)
            b = pltpu.roll(got_ref[s1 >> 1], (1 - (s1 & 1)) * 64, 1)
            full_ref[:, t * 128 : t * 128 + 128] = jnp.where(lane < FP, a, b)
        if chunk == 0:

            @pl.when(first >= 0)
            def _():
                diagonal = jnp.where((lane & 63) == iota((FP, 128), 0), qp_ref[...], 0.0)
                for t in range(2):
                    at = slice(t * 128, t * 128 + 128)
                    add = jnp.where(2 * t + (lane >> 6) == first, diagonal, 0.0)
                    full_ref[:, at] = (full_ref[:, at].astype(F32) + add).astype(BF16)

        at = pl.ds(chunk * tiles // chunks * 128, tiles // chunks * 128)
        copies.append(pltpu.make_async_copy(full_ref.at[:, at], out_ref.at[:, at], out_sems.at[chunk]))
        copies[-1].start()
    for copy in copies:
        copy.wait()


def shift(x, axis, size, by):
    return lax.ppermute(x, axis, [(i, (i + by) % size) for i in range(size)])


def along(x, by):
    pairs = [(z * NC + c, (z + (by if c == 0 else -by)) % NZ * NC + c) for z in range(NZ) for c in range(NC)]
    return lax.ppermute(x, ("z", "core"), pairs)


def body(coarse_kernel, row_intersection, col_intersection, row_nearest, col_nearest, qp_energy):
    y, z, core, band = (lax.axis_index(a) for a in ("y", "z", "core", "band"))
    near = [coarse_kernel] + [shift(coarse_kernel, "band", NB, d) for d in (2, 1, 3)]
    pick = (band - row_nearest) % NB
    c, v = row_intersection[0, 0], row_intersection[1, 0]
    row_coef = (c[:, None, :, None] * v[None, :, None, :]).reshape(FP, CP).astype(BF16)

    smem = pl.BlockSpec(memory_space=pltpu.SMEM)
    limit = pltpu.CompilerParams(vmem_limit_bytes=16 * 2**20)
    request, block = pl.pallas_call(
        request_kernel,
        in_specs=[smem] + whole(3),
        out_specs=whole(2),
        out_shape=[
            jax.ShapeDtypeStruct((GROUP, CAP, NZ, 768), BF16),
            jax.ShapeDtypeStruct((1, FC), jnp.int32),
        ],
        compiler_params=limit,
        name="request",
    )(
        z[None],
        col_nearest[None, :],
        col_intersection[0].reshape(FC, 96),
        col_intersection[1].reshape(FC, 96),
    )
    request, *near = lax.optimization_barrier((request, *near))
    request = lax.all_to_all(request, ("y", "core"), 0, 0, tiled=True)
    lanes = GROUP * CAP * FP
    *factors, local = pl.pallas_call(
        expand_kernel,
        in_specs=whole(1),
        out_specs=whole(5),
        out_shape=[
            *[jax.ShapeDtypeStruct((GROUP, NBC * HALF, 128), F32)] * 4,
            jax.ShapeDtypeStruct((NZ, lanes), F32),
        ],
        compiler_params=limit,
        name="expand",
    )(request)

    own = pl.pallas_call(
        strip_kernel,
        in_specs=[smem] + whole(5),
        out_specs=whole(1)[0],
        out_shape=jax.ShapeDtypeStruct((2, CP, 128), BF16),
        compiler_params=limit,
        cost_estimate=pl.CostEstimate(flops=0, bytes_accessed=0, transcendentals=0),
        name="strip",
    )(pick, *near, row_coef)

    own = jnp.concatenate([own, shift(own, "core", NC, 1)])
    one = along(own, 1)
    two = along(jnp.concatenate([own, one]), 2)
    four = along(two, 2)
    six = along(four, 2)
    eight = along(six[4:6], 1)
    strips = [own, one, two, four, six, eight]
    places = [(0, ((0, 0), (0, 1)))]
    for a, blocks in ((1, 2), (2, 4), (3, 4), (4, 4), (5, 1)):
        places += [(len(places) + b, ((a, 2 * b), (a, 2 * b + 1))) for b in range(blocks)]

    anywhere = pl.BlockSpec(memory_space=pl.ANY)
    got = []
    for n, (low, high) in enumerate(PARTS):
        results = []
        for lo, hi in RANGES[n]:
            used = sorted({a for _, pairs in places[lo:hi] for a, _ in pairs})
            halves = sorted({pos // HALF for pos in range(lo, hi)})
            mine = [(pos, tuple((used.index(a), b) for a, b in pairs)) for pos, pairs in places[lo:hi]]
            operands = [local, *[f for h in halves for f in factors[2 * h : 2 * h + 2]], *[strips[a] for a in used]]
            result = pl.pallas_call(
                functools.partial(result_kernel, mine, halves, lo - low),
                in_specs=whole(len(operands)) + [anywhere] * len(results),
                out_specs=anywhere,
                out_shape=jax.ShapeDtypeStruct((GROUP, high - low, FP, 128), BF16),
                input_output_aliases={len(operands): 0} if results else {},
                scratch_shapes=[pltpu.VMEM((hi - lo, GROUP, FP, 128), BF16), pltpu.SemaphoreType.DMA((hi - lo,))],
                compiler_params=limit,
                cost_estimate=pl.CostEstimate(flops=COSTS[lo] * 10**9, bytes_accessed=10**6, transcendentals=0),
                name="result",
            )(*operands, *results)
            results = [result]
            local, result = lax.optimization_barrier((local, result))
            results = [result]
        if got:
            result, got[-1] = lax.optimization_barrier((result, got[-1]))
        got.append(lax.all_to_all(result, ("y", "core"), 0, 0, tiled=True).reshape(-1, FP, 128))

    first = jnp.where((y == 0) & (z == 0) & (core == 0), band, -1)
    return pl.pallas_call(
        assemble_kernel,
        in_specs=[smem, smem, *[anywhere] * len(got), *whole(1)],
        out_specs=anywhere,
        out_shape=jax.ShapeDtypeStruct((FP, FC * FP), BF16),
        scratch_shapes=[
            pltpu.VMEM((GROUP * NZ, FP, 128), BF16),
            pltpu.VMEM((FP, FC * FP), BF16),
            pltpu.SemaphoreType.DMA((len(got),)),
            pltpu.SemaphoreType.DMA((12,)),
        ],
        compiler_params=limit,
        name="assemble",
    )(block.reshape(FC), first[None], *got, qp_energy[:, None])


def solution(mesh):
    fine = Mesh(mesh.devices.reshape(NY, NZ, NC, NB), ("y", "z", "core", "band"))
    kcol = ("y", "z", "core")
    return jax.shard_map(
        body,
        mesh=fine,
        in_specs=(
            P("band", kcol),
            P(None, "band", None, None),
            P(None, kcol, None, None),
            P("band"),
            P(kcol),
            P("band"),
        ),
        out_specs=P("band", kcol),
        check_vma=False,
    )
```

```python
import functools

import jax
import jax.numpy as jnp
from jax import lax
from jax.experimental import pallas as pl
from jax.experimental.pallas import tpu as pltpu
from jax.sharding import Mesh
from jax.sharding import PartitionSpec as P

NBF = 8
NBC = 12
FP = NBF * NBF
CP = NBC * NBC
RC = 4
NY, NZ, NC, NB = 4, 16, 2, 4
GROUP = NY * NC
FC = 144
HELD = 4
CAP = 2
PARTS = ((0, 5), (5, 11), (11, 16))
RANGES = (((0, 3), (3, 5)), ((5, 7), (7, 11)), ((11, 15), (15, 16)))
HALF = NZ // 2
COSTS = {0: 0, 3: 10, 5: 0, 7: 20, 11: 4, 15: 0}
F32 = jnp.float32
BF16 = jnp.bfloat16


def iota(shape, dim):
    return lax.broadcasted_iota(jnp.int32, shape, dim)


def dot(a, b, dims=((1,), (0,))):
    return lax.dot_general(a, b, (dims, ((), ())), preferred_element_type=F32)


def whole(n):
    return [pl.BlockSpec(memory_space=pltpu.VMEM)] * n


def strip_kernel(pick_ref, k0, k2, k1, k3, coef_ref, out_ref):
    pick = pick_ref[0]
    rows = jnp.where(pick == 0, k0[...], k1[...])
    rows = jnp.where(pick == 2, k2[...], rows)
    rows = jnp.where(pick == 3, k3[...], rows)
    strip = dot(rows, coef_ref[...], ((0,), (1,))).astype(BF16)
    to = iota((CP, CP), 0)
    low = (to >> 3) * NBC + (to & 7)
    high = ((to - 96) >> 2) * NBC + 8 + (to & 3)
    order = (jnp.where(to < 96, low, high) == iota((CP, CP), 1)).astype(BF16)
    for pair in range(2):
        at = pair * 2 * CP
        both = jnp.concatenate([strip[at : at + CP], strip[at + CP : at + 2 * CP]], axis=1)
        out_ref[pair] = dot(order, both).astype(BF16)


def request_kernel(z_ref, row_ref, conduction_ref, valence_ref, out_ref, block_ref):
    z = z_ref[0]
    near = row_ref[...]
    holder = near >> 2
    square = (FC, FC)
    here = iota(square, 0) == iota(square, 1)
    column = jnp.sum(jnp.where(here, near, 0), axis=1, keepdims=True)
    earlier = ((column >> 2) == holder) & (iota(square, 0) < iota(square, 1))
    rank = jnp.sum(earlier.astype(jnp.int32), axis=0, keepdims=True)
    rel = ((holder >> 1) - z) & (NZ - 1)
    far = jnp.minimum(rel, NZ - rel)
    core = holder & 1
    server = jnp.where((far & 7) == 0, core, (rel < 8).astype(jnp.int32))
    pos = jnp.where((far & 7) == 0, (far >> 3) * 15, 2 * far - 1 + (core ^ server))
    group = (holder >> 5) * NC + server
    slot = (group * NZ + pos) * CAP + rank
    block = jnp.zeros_like(pos)
    for lo, hi in PARTS:
        block = jnp.where((pos >= lo) & (pos < hi), lo * GROUP + group * (hi - lo) + pos - lo, block)
    block_ref[...] = block * CAP + rank
    lanes = 12 * 64
    source = iota((96, lanes), 0)
    lane = iota((96, lanes), 1)
    i, inner = lane >> 6, lane & 63
    spot = (inner & 7) * NBC + i
    table = jnp.zeros((FC, lanes), F32)
    for t, ref in enumerate((conduction_ref, valence_ref)):
        rest = ref[...]
        for s in range(3):
            term = rest.astype(BF16)
            rest = rest - term.astype(F32)
            place = ((source == spot) & ((inner >> 3) == s * 2 + t)).astype(BF16)
            table = table + dot(term, place)
    local = (column & 3).astype(F32)
    table = jnp.where((iota((FC, lanes), 1) & 63) == 48, local, table).astype(BF16)
    row = iota((GROUP * NZ, FC), 0) * CAP
    for r in range(CAP):
        one = (slot == row + r).astype(BF16)
        out_ref[:, r] = dot(one, table).astype(BF16).reshape(GROUP, NZ, lanes)


def expand_kernel(x_ref, u0_ref, v0_ref, u1_ref, v1_ref, local_ref):
    k = iota((256, 512), 0)
    n = iota((256, 512), 1)
    inner = k & 63
    want = jnp.where((n & 128) == 0, (n >> 3) & 7, n & 7)
    same = ((k >> 7) == ((n >> 6) & 1)) & (((k >> 6) & 1) == (n >> 8))
    same = same & (inner < 48) & (((inner >> 3) & 1) == ((n >> 7) & 1)) & ((inner & 7) == want)
    spread = same.astype(BF16)
    k = iota((256, 128), 0)
    n = iota((256, 128), 1)
    spread_local = (((k & 127) == 48) & ((k >> 7) == (n >> 6))).astype(BF16)
    for d in range(GROUP):
        lanes = pl.ds(d * 128, 128)
        for m in range(6):
            at = pl.ds(m * 128, 128)
            x = jnp.concatenate([x_ref[d, 0, :, at], x_ref[d, 1, :, at]], axis=1)
            y = dot(x, spread)
            for half in range(2):
                rows = pl.ds((m * 2 + half) * HALF, HALF)
                for n, (u_ref, v_ref) in enumerate(((u0_ref, v0_ref), (u1_ref, v1_ref))):
                    part = y[n * HALF : (n + 1) * HALF, half * 256 : half * 256 + 256]
                    u_ref[d, rows] = part[:, :128]
                    v_ref[d, rows] = part[:, 128:]
            if m == 0:
                local_ref[:, lanes] = dot(x, spread_local)


def coefficients(u_ref, v_ref, d, pos):
    u = [jnp.broadcast_to(u_ref[d, pl.ds(i * HALF + pos, 1)], (8, 128)) for i in range(NBC)]
    v_low = v_ref[d, pl.ds(pos, 8, stride=HALF)]
    v_high = v_ref[d, pl.ds(8 * HALF + pos, 4, stride=HALF)]
    v_high = jnp.concatenate([v_high, v_high], axis=0)
    first = iota((8, 128), 0) < 4
    parts = [v_low * u[i] for i in range(NBC)]
    parts += [v_high * jnp.where(first, u[i], u[i + 1]) for i in range(0, NBC, 2)]
    return jnp.concatenate(parts, axis=0).astype(BF16)


def result_kernel(places, halves, offset, local_ref, *refs):
    factors = {h: refs[2 * n : 2 * n + 2] for n, h in enumerate(halves)}
    strips, (out_ref, kept_ref, sems) = refs[2 * len(halves) : -3], refs[-3:]
    copies = []
    for at, (pos, pairs) in enumerate(places):
        blocks = [strips[a][b] for a, b in pairs]
        u_ref, v_ref = factors[pos // HALF]
        for chunk in range(4):
            lanes = pl.ds(chunk * 256, 256)
            coef = jnp.concatenate([coefficients(u_ref, v_ref, 2 * chunk + d, pos % HALF) for d in range(2)], axis=1)
            low = dot(blocks[0], coef, ((0,), (0,)))
            high = dot(blocks[1], coef, ((0,), (0,)))
            local = local_ref[pl.ds(pos, 1), lanes]
            res = jnp.where(local == 0, low[:FP], low[FP:])
            res = jnp.where(local == 2, high[:FP], res)
            res = jnp.where(local == 3, high[FP:], res).astype(BF16)
            for half in range(2):
                kept_ref[at, chunk * 2 + half] = res[:, half * 128 : half * 128 + 128]
        copies.append(pltpu.make_async_copy(kept_ref.at[at], out_ref.at[:, offset + at], sems.at[at]))
        copies[-1].start()
    for copy in copies:
        copy.wait()


def assemble_kernel(block_ref, where_ref, *refs):
    parts, (qp_ref, out_ref, got_ref, full_ref, in_sems, out_sems) = refs[: len(PARTS)], refs[len(PARTS) :]
    copies = []
    for n, (lo, hi) in enumerate(PARTS):
        at = pl.ds(lo * GROUP, (hi - lo) * GROUP)
        copies.append(pltpu.make_async_copy(parts[n], got_ref.at[at], in_sems.at[n]))
        copies[-1].start()
    for copy in copies:
        copy.wait()
    first = where_ref[0]
    lane = iota((FP, 128), 1)
    tiles = FC // 2
    chunks = out_sems.shape[0]
    copies = []
    for chunk in range(chunks):
        for t in range(chunk * tiles // chunks, (chunk + 1) * tiles // chunks):
            s0, s1 = block_ref[2 * t], block_ref[2 * t + 1]
            a = pltpu.roll(got_ref[s0 >> 1], (s0 & 1) * 64, 1)
            b = pltpu.roll(got_ref[s1 >> 1], (1 - (s1 & 1)) * 64, 1)
            full_ref[:, t * 128 : t * 128 + 128] = jnp.where(lane < FP, a, b)
        if chunk == 0:

            @pl.when(first >= 0)
            def _():
                diagonal = jnp.where((lane & 63) == iota((FP, 128), 0), qp_ref[...], 0.0)
                for t in range(2):
                    at = slice(t * 128, t * 128 + 128)
                    add = jnp.where(2 * t + (lane >> 6) == first, diagonal, 0.0)
                    full_ref[:, at] = (full_ref[:, at].astype(F32) + add).astype(BF16)

        at = pl.ds(chunk * tiles // chunks * 128, tiles // chunks * 128)
        copies.append(pltpu.make_async_copy(full_ref.at[:, at], out_ref.at[:, at], out_sems.at[chunk]))
        copies[-1].start()
    for copy in copies:
        copy.wait()


def shift(x, axis, size, by):
    return lax.ppermute(x, axis, [(i, (i + by) % size) for i in range(size)])


def along(x, by):
    pairs = [(z * NC + c, (z + (by if c == 0 else -by)) % NZ * NC + c) for z in range(NZ) for c in range(NC)]
    return lax.ppermute(x, ("z", "core"), pairs)


def body(coarse_kernel, row_intersection, col_intersection, row_nearest, col_nearest, qp_energy):
    y, z, core, band = (lax.axis_index(a) for a in ("y", "z", "core", "band"))
    near = [coarse_kernel] + [shift(coarse_kernel, "band", NB, d) for d in (2, 1, 3)]
    pick = (band - row_nearest) % NB
    c, v = row_intersection[0, 0], row_intersection[1, 0]
    row_coef = (c[:, None, :, None] * v[None, :, None, :]).reshape(FP, CP).astype(BF16)

    smem = pl.BlockSpec(memory_space=pltpu.SMEM)
    limit = pltpu.CompilerParams(vmem_limit_bytes=16 * 2**20)
    request, block = pl.pallas_call(
        request_kernel,
        in_specs=[smem] + whole(3),
        out_specs=whole(2),
        out_shape=[
            jax.ShapeDtypeStruct((GROUP, CAP, NZ, 768), BF16),
            jax.ShapeDtypeStruct((1, FC), jnp.int32),
        ],
        compiler_params=limit,
        name="request",
    )(
        z[None],
        col_nearest[None, :],
        col_intersection[0].reshape(FC, 96),
        col_intersection[1].reshape(FC, 96),
    )
    request, *near = lax.optimization_barrier((request, *near))
    request = lax.all_to_all(request, ("y", "core"), 0, 0, tiled=True)
    lanes = GROUP * CAP * FP
    *factors, local = pl.pallas_call(
        expand_kernel,
        in_specs=whole(1),
        out_specs=whole(5),
        out_shape=[
            *[jax.ShapeDtypeStruct((GROUP, NBC * HALF, 128), F32)] * 4,
            jax.ShapeDtypeStruct((NZ, lanes), F32),
        ],
        compiler_params=limit,
        name="expand",
    )(request)

    own = pl.pallas_call(
        strip_kernel,
        in_specs=[smem] + whole(5),
        out_specs=whole(1)[0],
        out_shape=jax.ShapeDtypeStruct((2, CP, 128), BF16),
        compiler_params=limit,
        cost_estimate=pl.CostEstimate(flops=0, bytes_accessed=0, transcendentals=0),
        name="strip",
    )(pick, *near, row_coef)

    own = jnp.concatenate([own, shift(own, "core", NC, 1)])
    one = along(own, 1)
    two = along(jnp.concatenate([own, one]), 2)
    four = along(two, 2)
    six = along(four, 2)
    eight = along(six[4:6], 1)
    strips = [own, one, two, four, six, eight]
    places = [(0, ((0, 0), (0, 1)))]
    for a, blocks in ((1, 2), (2, 4), (3, 4), (4, 4), (5, 1)):
        places += [(len(places) + b, ((a, 2 * b), (a, 2 * b + 1))) for b in range(blocks)]

    anywhere = pl.BlockSpec(memory_space=pl.ANY)
    got = []
    for n, (low, high) in enumerate(PARTS):
        results = []
        for lo, hi in RANGES[n]:
            used = sorted({a for _, pairs in places[lo:hi] for a, _ in pairs})
            halves = sorted({pos // HALF for pos in range(lo, hi)})
            mine = [(pos, tuple((used.index(a), b) for a, b in pairs)) for pos, pairs in places[lo:hi]]
            operands = [local, *[f for h in halves for f in factors[2 * h : 2 * h + 2]], *[strips[a] for a in used]]
            result = pl.pallas_call(
                functools.partial(result_kernel, mine, halves, lo - low),
                in_specs=whole(len(operands)) + [anywhere] * len(results),
                out_specs=anywhere,
                out_shape=jax.ShapeDtypeStruct((GROUP, high - low, FP, 128), BF16),
                input_output_aliases={len(operands): 0} if results else {},
                scratch_shapes=[pltpu.VMEM((hi - lo, GROUP, FP, 128), BF16), pltpu.SemaphoreType.DMA((hi - lo,))],
                compiler_params=limit,
                cost_estimate=pl.CostEstimate(flops=COSTS[lo] * 10**9, bytes_accessed=10**6, transcendentals=0),
                name="result",
            )(*operands, *results)
            results = [result]
            local, result = lax.optimization_barrier((local, result))
            results = [result]
        if got:
            result, got[-1] = lax.optimization_barrier((result, got[-1]))
        got.append(lax.all_to_all(result, ("y", "core"), 0, 0, tiled=True).reshape(-1, FP, 128))

    first = jnp.where((y == 0) & (z == 0) & (core == 0), band, -1)
    return pl.pallas_call(
        assemble_kernel,
        in_specs=[smem, smem, *[anywhere] * len(got), *whole(1)],
        out_specs=anywhere,
        out_shape=jax.ShapeDtypeStruct((FP, FC * FP), BF16),
        scratch_shapes=[
            pltpu.VMEM((GROUP * NZ, FP, 128), BF16),
            pltpu.VMEM((FP, FC * FP), BF16),
            pltpu.SemaphoreType.DMA((len(got),)),
            pltpu.SemaphoreType.DMA((12,)),
        ],
        compiler_params=limit,
        name="assemble",
    )(block.reshape(FC), first[None], *got, qp_energy[:, None])


def solution(mesh):
    fine = Mesh(mesh.devices.reshape(NY, NZ, NC, NB), ("y", "z", "core", "band"))
    kcol = ("y", "z", "core")
    return jax.shard_map(
        body,
        mesh=fine,
        in_specs=(
            P("band", kcol),
            P(None, "band", None, None),
            P(None, kcol, None, None),
            P("band"),
            P(kcol),
            P("band"),
        ),
        out_specs=P("band", kcol),
        check_vma=False,
    )
```
